32 devices in a mesh: dp: 8 (over z, y), mod: 4 (over x, core).
Axes of the slice: x: 2, y: 2, z: 4, core: 2. Of those that a mesh axis runs over, the one named last changes fastest.
Arguments:
- embeddings: bfloat16 [4, 2048, 512], P('mod', 'dp'), may hold values from -4 to 4
- pairings: int32 [3, 4], replicated, may hold values from 0 to 3, as said below
- logit_scale: float32 [3], replicated, may hold values from 2 to 6
Outputs:
- gradient: float32 [4, 2048, 512], P('mod', 'dp')
- losses: float32 [4, 2048], P('mod', 'dp')
The draws below stay inside these ranges and needn't reach their ends.
Inputs may be any that keep to these rules, and one draw needn't show every extreme that they name: Row k of pairings maps each modality to its partner in matching k; each row is an involution without fixed points, and the three rows are the three perfect matchings of the four modalities in some order.
All inputs are finite; a program needn't handle non-finite values.
Results may differ from the reference program's by a relative error of at most 0.0013.
Values may be sent and summed in bfloat16 or wider, within the bound.
No kernel may reach another device: no remote copies, remote signals or barrier semaphores. Data moves between devices by JAX's collectives and lax.ppermute only.
A program may use at most 192 MiB of HBM per device.

```python
import math
import jax
import jax.numpy as jnp
from jax import lax

D = 512
CLIP_DEV = 256
CLIPS = 2048
N_DP = 8


def draw_pairings(key, part):
    order = jax.random.permutation(jax.random.fold_in(key, 3), 3).astype(jnp.int32)
    modal = jnp.arange(4, dtype=jnp.int32)
    return jnp.bitwise_xor(modal[None, :], order[:, None] + 1).astype(jnp.int32)


def draw_embeddings(key, part):
    normed = D ** (-0.25)
    base = jnp.clip(jax.random.normal(jax.random.fold_in(key, 21), (4, CLIPS, D), jnp.float32), -5.0, 5.0) * normed
    return jnp.clip(base, -4.0, 4.0).astype(jnp.bfloat16)


def setup_inputs(seed: int = 0) -> dict:
    arg_keys = jax.random.split(jax.random.key(seed), 4)
    return {
        "embeddings": draw_embeddings(jax.random.fold_in(arg_keys[3], 71), 0),
        "pairings": draw_pairings(jax.random.fold_in(arg_keys[3], 71), 0),
        "logit_scale": jnp.clip(jnp.exp(jax.random.uniform(arg_keys[2], (3,), jnp.float32, math.log(2.0), math.log(6.0))), 2.0, 6.0),
    }


def score_block(anchor_rows, partner, factor):
    return factor * lax.dot_general(anchor_rows, partner, (((1,), (1,)), ((), ())), preferred_element_type=jnp.float32)


def pair_terms(anchor, partner, factor):
    anchor_blocks = anchor.reshape(N_DP, CLIP_DEV, D)
    partner_blocks = partner.reshape(N_DP, CLIP_DEV, D)

    def block_max(rows_in):
        return jnp.max(score_block(rows_in, partner, factor), 0)

    col_max = jnp.max(lax.map(block_max, anchor_blocks), 0)

    def block_sum(rows_in):
        return jnp.sum(jnp.exp(score_block(rows_in, partner, factor) - col_max[None, :]), 0)

    col_lse = col_max + jnp.log(jnp.sum(lax.map(block_sum, anchor_blocks), 0))

    def block_terms(pair_in):
        rows_in, own_rows = pair_in
        scores = score_block(rows_in, partner, factor)
        row_max = jnp.max(scores, 1, keepdims=True)
        row_lse = row_max[:, 0] + jnp.log(jnp.sum(jnp.exp(scores - row_max), 1))
        weights = (jnp.exp(scores - row_lse[:, None]) + jnp.exp(scores - col_lse[None, :])).astype(jnp.bfloat16)
        product = jnp.dot(weights, partner, preferred_element_type=jnp.float32)
        own_float = own_rows.astype(jnp.float32)
        diagonal = factor * jnp.sum(rows_in.astype(jnp.float32) * own_float, -1)
        return factor * (product - 2.0 * own_float), row_lse - diagonal

    grad_blocks, loss_blocks = lax.map(block_terms, (anchor_blocks, partner_blocks))
    return grad_blocks.reshape(CLIPS, D), loss_blocks.reshape(CLIPS)


def reference(embeddings, pairings, logit_scale):
    grad_list = []
    loss_list = []
    for modality in range(4):
        grad_total = jnp.zeros((CLIPS, D), jnp.float32)
        loss_total = jnp.zeros((CLIPS,), jnp.float32)
        for matching in range(3):
            partner_id = pairings[matching, modality].astype(jnp.int32)
            partner = lax.dynamic_index_in_dim(embeddings, partner_id, 0, keepdims=False)
            grad_part, loss_part = pair_terms(embeddings[modality], partner, logit_scale[matching])
            grad_total = grad_total + grad_part
            loss_total = loss_total + loss_part
        grad_list.append(grad_total)
        loss_list.append(loss_total)
    return (jnp.stack(grad_list), jnp.stack(loss_list))
```

```python
import functools
import math

import jax
import jax.numpy as jnp
from jax import lax
from jax.experimental import pallas as pl
from jax.experimental.pallas import tpu as pltpu
from jax.sharding import PartitionSpec as P

LOG2E = math.log2(math.e)
TILE = 256
NT = (((1,), (1,)), ((), ()))


def fold(x):
    return x.reshape(x.shape[0] // 8, 8, x.shape[1])


def scores(rows, cols):
    return lax.dot_general(rows, cols, NT, preferred_element_type=jnp.float32)


def fetch_all(refs, scratch, sems):
    size = refs[0].shape[0]
    copies = []
    for i, ref in enumerate(refs):
        copy = pltpu.make_async_copy(ref, scratch.at[pl.ds(i * size, size)], sems.at[i])
        copy.start()
        copies.append(copy)
    return copies


def col_kernel(n_cols, factor_ref, *refs):
    row_refs, col_refs = refs[:8], refs[8 : 8 + n_cols]
    out_ref, rows, cols, row_sems, col_sems = refs[8 + n_cols :]
    size = row_refs[0].shape[0]
    copies = fetch_all(row_refs, rows, row_sems) + fetch_all(col_refs, cols, col_sems)
    for copy in copies:
        copy.wait()
    chunks = rows.shape[0] // TILE
    per_block = size // TILE

    def body(j, _):
        block = cols[pl.ds(pl.multiple_of(j * TILE, TILE), TILE), :]
        scale = factor_ref[j // (8 * per_block)] * LOG2E

        def group(g, carry):
            top, total = carry
            for i in range(8):
                start = pl.multiple_of(g * (8 * TILE) + i * TILE, TILE)
                s = fold(scores(rows[pl.ds(start, TILE), :], block))
                new = jnp.maximum(top, jnp.max(s, 0))
                shift = new * scale
                total = total * jnp.exp2(top * scale - shift) + jnp.sum(jnp.exp2(s * scale - shift[None]), 0)
                top = new
            return top, total

        carry = (jnp.full((8, TILE), -1e30, jnp.float32), jnp.zeros((8, TILE), jnp.float32))
        if chunks == 8:
            top, total = group(0, carry)
        else:
            top, total = lax.fori_loop(0, chunks // 8, group, carry)
        best = jnp.max(top, 0, keepdims=True)
        total = jnp.sum(total * jnp.exp2((top - best) * scale), 0, keepdims=True)
        out_ref[j] = best * scale + jnp.log2(total)
        return 0

    lax.fori_loop(0, cols.shape[0] // TILE, body, 0)


def col_stats(factors, rows, cols):
    size, width = rows[0].shape
    n_cols = len(cols)
    n_tiles = n_cols * size // TILE
    need = (8 + n_cols) * size * width * 2
    work = 8 * size * n_cols * size
    return pl.pallas_call(
        functools.partial(col_kernel, n_cols),
        out_shape=jax.ShapeDtypeStruct((n_tiles, 1, TILE), jnp.float32),
        in_specs=[pl.BlockSpec(memory_space=pltpu.SMEM)] + [pl.BlockSpec(memory_space=pl.ANY)] * (8 + n_cols),
        out_specs=pl.BlockSpec(memory_space=pltpu.VMEM),
        scratch_shapes=[
            pltpu.VMEM((8 * size, width), jnp.bfloat16),
            pltpu.VMEM((n_cols * size, width), jnp.bfloat16),
            pltpu.SemaphoreType.DMA((8,)),
            pltpu.SemaphoreType.DMA((n_cols,)),
        ],
        compiler_params=pltpu.CompilerParams(vmem_limit_bytes=need + (12 << 20)),
        cost_estimate=pl.CostEstimate(flops=2 * work * width, bytes_accessed=need, transcendentals=work),
        name="col_stats",
    )(factors, *rows, *cols)


def final_kernel(factor_ref, own_ref, pown1, pown2, pown3, lse_ref, *refs):
    col_refs = refs[:24]
    grad_ref, loss_ref, cols, prob, colprob, sems = refs[24:]
    size = col_refs[0].shape[0]
    groups = size // TILE
    copies = fetch_all(col_refs, cols, sems)
    own = own_ref[...]
    own_float = own.astype(jnp.float32)
    grad = jnp.zeros(own.shape, jnp.float32)
    loss = jnp.zeros((own.shape[0], 1), jnp.float32)
    n = own.shape[0]

    def loop(f, carry):
        if groups == 1:
            for i in range(8):
                carry = f(i, carry)
            return carry

        def eight(g, c):
            for i in range(8):
                c = f(g * 8 + i, c)
            return c

        return lax.fori_loop(0, groups, eight, carry)

    for pair, pown_ref in enumerate((pown1, pown2, pown3)):
        slot = pair if groups == 1 else 0
        factor = factor_ref[pair]
        scale = factor * LOG2E
        for copy in copies[8 * pair : 8 * pair + 8]:
            copy.wait()

        def block_of(j):
            return cols[pl.ds(pl.multiple_of((pair * 8 * groups + j) * TILE, TILE), TILE), :]

        def first(j, top):
            s = scores(own, block_of(j))
            prob[slot, j] = s
            return jnp.maximum(top, jnp.maximum(s[:, :128], s[:, 128:]))

        top = loop(first, jnp.full((n, 128), -1e30, jnp.float32))
        best = jnp.max(top, 1, keepdims=True) * scale

        def second(j, total):
            s = prob[slot, j] * scale
            p = jnp.exp2(s - best)
            prob[slot, j] = p
            colprob[slot, j] = jnp.exp2(s - lse_ref[pair * 8 * groups + j])
            return total + p[:, :128] + p[:, 128:]

        total = jnp.sum(loop(second, jnp.zeros((n, 128), jnp.float32)), 1, keepdims=True)
        inverse = 1.0 / total

        def third(j, acc):
            w = (prob[slot, j] * inverse + colprob[slot, j]).astype(jnp.bfloat16)
            return acc + jnp.dot(w, block_of(j), preferred_element_type=jnp.float32)

        product = loop(third, jnp.zeros(own.shape, jnp.float32))
        partner = pown_ref[...].astype(jnp.float32)
        grad = grad + factor * (product - 2.0 * partner)
        diagonal = factor * jnp.sum(own_float * partner, 1, keepdims=True)
        loss = loss + (best * (1.0 / LOG2E) + jnp.log(total) - diagonal)
    grad_ref[...] = grad
    loss_ref[...] = jnp.transpose(jnp.broadcast_to(loss, (n, 128)))[:8, :]


def final(factors, own, pown, lse, cols):
    n, width = own.shape
    size = cols[0].shape[0]
    groups = size // TILE
    slots = 3 if groups == 1 else 1
    need = 24 * size * width * 2 + slots * 8 * groups * n * TILE * 8
    vmem = pl.BlockSpec(memory_space=pltpu.VMEM)
    return pl.pallas_call(
        final_kernel,
        out_shape=(jax.ShapeDtypeStruct((n, width), jnp.float32), jax.ShapeDtypeStruct((8, n), jnp.float32)),
        in_specs=[pl.BlockSpec(memory_space=pltpu.SMEM)] + [vmem] * 5 + [pl.BlockSpec(memory_space=pl.ANY)] * 24,
        out_specs=(vmem, vmem),
        scratch_shapes=[
            pltpu.VMEM((24 * size, width), jnp.bfloat16),
            pltpu.VMEM((slots, 8 * groups, n, TILE), jnp.float32),
            pltpu.VMEM((slots, 8 * groups, n, TILE), jnp.float32),
            pltpu.SemaphoreType.DMA((24,)),
        ],
        compiler_params=pltpu.CompilerParams(vmem_limit_bytes=need + (12 << 20)),
        cost_estimate=pl.CostEstimate(flops=4 * n * 24 * size * width, bytes_accessed=need, transcendentals=2 * n * 24 * size),
        name="weights_and_gradient",
    )(factors, own, *pown, lse, *cols)


def shards(n_dp, embeddings, pairings, logit_scale):
    own = embeddings[0]
    n = own.shape[0]
    group = n_dp // 8
    dp_index = lax.axis_index("dp")
    mod_index = lax.axis_index("mod")

    def send(block, dp_xor, mod_xor):
        pairs = [
            (d * 4 + m, (d ^ (dp_xor * group)) * 4 + (m ^ mod_xor)) for d in range(n_dp) for m in range(4)
        ]
        return lax.ppermute(block, ("dp", "mod"), pairs)

    block = own
    if group > 1:
        members = [[g * group + i for i in range(group)] for g in range(8)]
        block = lax.all_gather(own, "dp", axis=0, tiled=True, axis_index_groups=members)

    e = [[None] * 8 for _ in range(4)]
    e[0][0] = block
    e[2][0] = send(e[0][0], 0, 2)
    e[0][1] = send(e[0][0], 1, 0)
    e[0][2] = send(e[0][0], 2, 0)
    e[0][4] = send(e[0][0], 4, 0)
    e[2][1] = send(e[0][1], 0, 2)
    e[0][3] = send(e[0][2], 1, 0)
    e[0][6] = send(e[0][4], 2, 0)
    e[2][4] = send(e[0][4], 0, 2)
    e[0][5] = send(e[0][4], 1, 0)
    e[2][2] = send(e[2][0], 2, 0)
    e[2][6] = send(e[0][6], 0, 2)
    e[0][7] = send(e[0][6], 1, 0)
    e[2][5] = send(e[0][5], 0, 2)
    e[2][3] = send(e[2][1], 2, 0)
    e[2][7] = send(e[2][6], 1, 0)
    for a in range(8):
        e[1][a] = send(e[0][a], 0, 1)
        e[3][a] = send(e[2][a], 0, 1)

    partner_ids = lax.dynamic_index_in_dim(pairings, mod_index, 1, keepdims=False)
    factors = jnp.stack(
        [jnp.sum(jnp.where(partner_ids == (mod_index ^ m), logit_scale, 0.0)) for m in (1, 2, 3)]
    )
    pown = [e[m][0] for m in (1, 2, 3)]
    if group > 1:
        start = (dp_index % group) * n
        pown = [lax.dynamic_slice_in_dim(x, start, n, 0) for x in pown]
    cols = e[1] + e[2] + e[3]
    lse = col_stats(factors, e[0], cols)
    gradient, losses = final(factors, own, pown, lse, cols)
    return gradient[None], losses[:1]


def solution(mesh):
    return jax.shard_map(
        functools.partial(shards, mesh.shape["dp"]),
        mesh=mesh,
        in_specs=(P("mod", "dp", None), P(), P()),
        out_specs=(P("mod", "dp", None), P("mod", "dp")),
        check_vma=False,
    )
```

```python
import functools
CONFIG = {'route': {'a1': ('a0', 'Y'), 'a2': ('a0', 'Z'), 'a4': ('a0', 'W'), 'b0': ('a0', 'X'), 'b1': ('a1', 'X'), 'a3': ('a2', 'Y'), 'a6': ('a4', 'Z'), 'b4': ('a4', 'X'), 'a5': ('a4', 'Y'), 'b2': ('b0', 'Z'), 'b6': ('a6', 'X'), 'a7': ('a6', 'Y'), 'b3': ('b1', 'Z'), 'b5': ('a5', 'X'), 'b7': ('b6', 'Y')}, 'ties': {'a3': ['b0'], 'a6': ['b1'], 'b4': ['b1'], 'a5': ['a3'], 'b2': ['b1'], 'b6': ['b4'], 'a7': ['a5'], 'b3': ['a7'], 'b5': ['b6'], 'P4': ['b7'], 'P5': ['K1']}, 'packs': {'P1': ['a1', 'a2', 'a4', 'b0'], 'P2': ['a3', 'a6', 'b1'], 'P3': ['a5', 'b4', 'b2'], 'P0': ['a0'], 'P5': ['b6'], 'P6': ['a7'], 'P4': ['b3', 'b5'], 'P7': ['b7']}, 'kernels': {'K1': (['a0', 'a1', 'a2', 'a4', 'a3', 'a6'], ['b0', 'c0', 'c2', 'c4', 'd0']), 'K2': (['a5'], ['c6', 'b4', 'b2']), 'K3': (['a7'], ['d4', 'd2', 'b6', 'd6'])}, 'cost': {'K1': 40, 'K2': 40, 'K3': 40}, 'emit': ['a2', 'a4', 'a1', 'b0', 'b1', 'a3', 'a6', 'b4', 'a5', 'b2', 'b6', 'a7', 'b3', 'b5', 'b7']}
import math

import jax
import jax.numpy as jnp
from jax import lax
from jax.experimental import pallas as pl
from jax.experimental.pallas import tpu as pltpu
from jax.sharding import PartitionSpec as P

LOG2E = math.log2(math.e)
TILE = 256
NT = (((1,), (1,)), ((), ()))
SMEM = pl.BlockSpec(memory_space=pltpu.SMEM)
VMEM = pl.BlockSpec(memory_space=pltpu.VMEM)
LIGHT = pl.CostEstimate(flops=1000, bytes_accessed=1000, transcendentals=0)


def scores(rows, cols):
    return lax.dot_general(rows, cols, NT, preferred_element_type=jnp.float32)


def factor_kernel(pairings_ref, scale_ref, out_ref):
    mine = lax.axis_index("mod")
    for m in (1, 2, 3):
        factor = jnp.float32(0.0)
        for k in range(3):
            factor = factor + jnp.where(pairings_ref[k, mine] == (mine ^ m), scale_ref[k], 0.0)
        out_ref[m - 1] = jnp.full(out_ref.shape[1:], factor, jnp.float32)
        out_ref[m + 2] = jnp.full(out_ref.shape[1:], factor * LOG2E, jnp.float32)


def pair_factors(pairings, logit_scale, size):
    return pl.pallas_call(
        factor_kernel,
        out_shape=jax.ShapeDtypeStruct((6, 8, size), jnp.float32),
        in_specs=[SMEM] * 2,
        out_specs=VMEM,
        compiler_params=pltpu.CompilerParams(vmem_limit_bytes=1 << 20),
        cost_estimate=LIGHT,
        name="pair_factors",
    )(pairings, logit_scale)


def unique(blocks):
    arrays, places = [], []
    for array, slab in blocks:
        for i, known in enumerate(arrays):
            if known is array:
                break
        else:
            i = len(arrays)
            arrays.append(array)
        places.append((i, slab))
    return arrays, places


class Placed:
    def __init__(self, ref, slab, size):
        self.ref, self.start, self.size = ref, slab * size, size

    def all(self):
        return self.ref[pl.ds(self.start, self.size), :]

    def part(self, i):
        return self.ref[pl.ds(pl.multiple_of(self.start + i * TILE, TILE), TILE), :]


def stats_kernel(size, places, n_arrays, plan, n_rows, n_old, order, n_stack, factor_ref, *refs):
    blocks = [Placed(refs[i], slab, size) for i, slab in places]
    rows, cols, stack = blocks[:n_rows], blocks[n_rows : n_rows + len(plan)], blocks[n_rows + len(plan) :]
    refs = refs[n_arrays:]
    old = refs[:2] if n_old else None
    outs = refs[2 if n_old else 0 :]
    for i, block in enumerate(stack):
        outs[-1][i * size : (i + 1) * size, :] = block.all()
    for c, (m, members) in enumerate(plan):
        scale = factor_ref[m + 2]
        if c < n_old:
            top, total = old[0][c], old[1][c]
        else:
            top = jnp.full((8, size), -1e30, jnp.float32)
            total = jnp.zeros((8, size), jnp.float32)
        block = cols[c].all()
        for r in members:

            def chunk(i, carry, r=r, block=block, scale=scale):
                top, total = carry
                s = scores(rows[r].part(i), block)
                s = s.reshape(TILE // 8, 8, size)
                new = jnp.maximum(top, jnp.max(s, 0))
                shift = new * scale
                total = total * jnp.exp2(top * scale - shift) + jnp.sum(jnp.exp2(s * scale[None] - shift[None]), 0)
                return new, total

            if size == TILE:
                top, total = chunk(0, (top, total))
            else:
                top, total = lax.fori_loop(0, size // TILE, chunk, (top, total))
        if order:
            best = jnp.max(top, 0, keepdims=True)
            total = jnp.sum(total * jnp.exp2((top - best) * scale), 0, keepdims=True)
            outs[0][order[c]] = best * scale[:1] + jnp.log2(total)
        else:
            outs[0][c] = top
            outs[1][c] = total


def stats(info, size, rows, cols, plan, old=None, order=None, stack=(), cost=4):
    arrays, places = unique(list(rows) + list(cols) + list(stack))
    width = arrays[0].shape[1]
    n = len(plan)
    n_old = old[0].shape[0] if old else 0
    state = jax.ShapeDtypeStruct((n, 8, size), jnp.float32)
    out = [jax.ShapeDtypeStruct((n, 1, size), jnp.float32)] if order else [state, state]
    if stack:
        out.append(jax.ShapeDtypeStruct((len(stack) * size, width), jnp.bfloat16))
    tiles = sum(len(members) for _, members in plan)
    used = sum(math.prod(x.shape) * 2 for x in arrays) + len(stack) * size * width * 2
    return pl.pallas_call(
        functools.partial(
            stats_kernel, size, tuple(places), len(arrays), plan, len(rows), n_old, order, len(stack)
        ),
        out_shape=tuple(out),
        in_specs=[VMEM] * (1 + len(arrays) + (2 if old else 0)),
        out_specs=tuple([VMEM] * len(out)),
        compiler_params=pltpu.CompilerParams(vmem_limit_bytes=(6 << 20) + (used if size > TILE else 0)),
        cost_estimate=pl.CostEstimate(flops=cost * tiles * size * size * width, bytes_accessed=1000, transcendentals=0),
        name="col_stats",
    )(info, *arrays, *(old or ()))


def pack_kernel(*refs):
    size = refs[0].shape[0]
    for i, ref in enumerate(refs[:-1]):
        refs[-1][i * size : (i + 1) * size, :] = ref[...]


def pack(*blocks):
    size, width = blocks[0].shape
    return pl.pallas_call(
        pack_kernel,
        out_shape=jax.ShapeDtypeStruct((len(blocks) * size, width), blocks[0].dtype),
        in_specs=[VMEM] * len(blocks),
        out_specs=VMEM,
        compiler_params=pltpu.CompilerParams(vmem_limit_bytes=(2 << 20) + (len(blocks) * size * width * 4 if size > TILE else 0)),
        cost_estimate=LIGHT,
        name="pack",
    )(*blocks)


def own_kernel(places, n_arrays, factor_ref, own_ref, lse_ref, *refs):
    blocks = [Placed(refs[i], slab, TILE) for i, slab in places]
    cols, pown = blocks[:24], blocks[24:]
    grad_ref, loss_ref, prob, score, scratch = refs[n_arrays:]
    own = own_ref[...]
    own_float = own.astype(jnp.float32)
    n = own.shape[0]
    grad = jnp.zeros(own.shape, jnp.float32)
    loss = jnp.zeros((n, 1), jnp.float32)
    for pair in range(3):
        factor = factor_ref[pair, :1, :1]
        scale = factor_ref[pair + 3, :1]
        held = [(scratch if a % 2 == 0 else score).at[pair * 4 + a // 2] for a in range(8)]
        top = jnp.full((n, 128), -1e30, jnp.float32)
        for a in range(8):
            s = scores(own, cols[pair * 8 + a].all())
            held[a][...] = s
            top = jnp.maximum(top, jnp.maximum(s[:, :128], s[:, 128:]))
        best = jnp.max(top, 1, keepdims=True) * scale[:, :1]
        total = jnp.zeros((n, 128), jnp.float32)
        for a in range(8):
            p = jnp.exp2(held[a][...] * scale - best)
            prob[pair * 8 + a] = p
            total = total + p[:, :128] + p[:, 128:]
        total = jnp.sum(total, 1, keepdims=True)
        inverse = 1.0 / total
        product = jnp.zeros(own.shape, jnp.float32)
        for a in range(8):
            p = prob[pair * 8 + a] * inverse
            if a % 2:
                prob[pair * 8 + a] = p
                continue
            w = (p + jnp.exp2(held[a][...] * scale - lse_ref[pair * 4 + a // 2])).astype(jnp.bfloat16)
            product = product + jnp.dot(w, cols[pair * 8 + a].all(), preferred_element_type=jnp.float32)
        partner = pown[pair].all().astype(jnp.float32)
        grad = grad + factor * (product - 2.0 * partner)
        diagonal = factor * jnp.sum(own_float * partner, 1, keepdims=True)
        loss = loss + (best * (1.0 / LOG2E) + jnp.log(total) - diagonal)
    grad_ref[...] = grad
    loss_ref[...] = jnp.transpose(jnp.broadcast_to(loss, (n, 128)))[:1, :]


def own_half(info, own, lse, cols, pown):
    arrays, places = unique(cols + pown)
    n, width = own.shape
    return pl.pallas_call(
        functools.partial(own_kernel, tuple(places), len(arrays)),
        out_shape=(
            jax.ShapeDtypeStruct((n, width), jnp.float32),
            jax.ShapeDtypeStruct((1, n), jnp.float32),
            jax.ShapeDtypeStruct((24, n, TILE), jnp.float32),
            jax.ShapeDtypeStruct((12, n, TILE), jnp.float32),
        ),
        in_specs=[VMEM] * (3 + len(arrays)),
        out_specs=(VMEM,) * 4,
        scratch_shapes=[pltpu.VMEM((12, n, TILE), jnp.float32)],
        compiler_params=pltpu.CompilerParams(vmem_limit_bytes=12 * n * TILE * 4 + (6 << 20)),
        cost_estimate=LIGHT,
        name="own_half",
    )(info, own, lse, *arrays)


def other_kernel(places, n_arrays, factor_ref, half_ref, prob, score, lse_ref, *refs):
    cols = [Placed(refs[i], slab, TILE) for i, slab in places]
    grad = half_ref[...]
    for pair in range(3):
        scale = factor_ref[pair + 3, :1]
        product = jnp.zeros(half_ref.shape, jnp.float32)
        for i in range(4):
            q = jnp.exp2(score[pair * 4 + i] * scale - lse_ref[pair * 4 + i])
            w = (prob[pair * 8 + 2 * i + 1] + q).astype(jnp.bfloat16)
            product = product + jnp.dot(w, cols[pair * 4 + i].all(), preferred_element_type=jnp.float32)
        grad = grad + factor_ref[pair, :1, :1] * product
    refs[n_arrays][...] = grad


def other_half(info, half, prob, score, lse, cols):
    arrays, places = unique(cols)
    return pl.pallas_call(
        functools.partial(other_kernel, tuple(places), len(arrays)),
        out_shape=jax.ShapeDtypeStruct(half.shape, jnp.float32),
        in_specs=[VMEM] * (5 + len(arrays)),
        out_specs=VMEM,
        compiler_params=pltpu.CompilerParams(vmem_limit_bytes=8 << 20),
        cost_estimate=LIGHT,
        name="other_half",
    )(info, half, prob, score, lse, *arrays)


def whole_kernel(size, places, n_arrays, factor_ref, own_ref, *refs):
    cols = [Placed(refs[i], slab, size) for i, slab in places]
    pown = refs[n_arrays : n_arrays + 3]
    lses = refs[n_arrays + 3 : n_arrays + 5]
    grad_ref, loss_ref, prob, colprob = refs[n_arrays + 5 :]
    groups = size // TILE
    own = own_ref[...]
    own_float = own.astype(jnp.float32)
    n = own.shape[0]
    grad = jnp.zeros(own.shape, jnp.float32)
    loss = jnp.zeros((n, 1), jnp.float32)

    def loop(f, carry):
        for a in range(8):
            carry = lax.fori_loop(0, groups, functools.partial(f, a), carry)
        return carry

    for pair in range(3):
        factor = factor_ref[pair, :1, :1]
        scale = factor_ref[pair + 3, :1, :TILE]

        def first(a, g, top, pair=pair):
            s = scores(own, cols[pair * 8 + a].part(g))
            prob[a * groups + g] = s
            return jnp.maximum(top, jnp.maximum(s[:, :128], s[:, 128:]))

        top = loop(first, jnp.full((n, 128), -1e30, jnp.float32))
        best = jnp.max(top, 1, keepdims=True) * scale[:, :1]

        def second(a, g, total, pair=pair, best=best, scale=scale):
            j = a * groups + g
            s = prob[j] * scale
            p = jnp.exp2(s - best)
            prob[j] = p
            lse = lses[a % 2][pair * 4 + a // 2, :, pl.ds(pl.multiple_of(g * TILE, TILE), TILE)]
            colprob[j] = jnp.exp2(s - lse)
            return total + p[:, :128] + p[:, 128:]

        total = jnp.sum(loop(second, jnp.zeros((n, 128), jnp.float32)), 1, keepdims=True)
        inverse = 1.0 / total

        def third(a, g, acc, pair=pair, inverse=inverse):
            j = a * groups + g
            w = (prob[j] * inverse + colprob[j]).astype(jnp.bfloat16)
            return acc + jnp.dot(w, cols[pair * 8 + a].part(g), preferred_element_type=jnp.float32)

        product = loop(third, jnp.zeros(own.shape, jnp.float32))
        partner = pown[pair][...].astype(jnp.float32)
        grad = grad + factor * (product - 2.0 * partner)
        diagonal = factor * jnp.sum(own_float * partner, 1, keepdims=True)
        loss = loss + (best * (1.0 / LOG2E) + jnp.log(total) - diagonal)
    grad_ref[...] = grad
    loss_ref[...] = jnp.transpose(jnp.broadcast_to(loss, (n, 128)))[:1, :]


def whole(info, size, own, pown, lse, lse_other, cols):
    arrays, places = unique(cols)
    n, width = own.shape
    slots = 8 * size // TILE
    scratch = pltpu.VMEM((slots, n, TILE), jnp.float32)
    need = 24 * size * width * 2 + slots * n * TILE * 8
    return pl.pallas_call(
        functools.partial(whole_kernel, size, tuple(places), len(arrays)),
        out_shape=(jax.ShapeDtypeStruct((n, width), jnp.float32), jax.ShapeDtypeStruct((1, n), jnp.float32)),
        in_specs=[VMEM] * (7 + len(arrays)),
        out_specs=(VMEM, VMEM),
        scratch_shapes=[scratch, scratch],
        compiler_params=pltpu.CompilerParams(vmem_limit_bytes=need + (6 << 20)),
        cost_estimate=LIGHT,
        name="weights_and_gradient",
    )(info, own, *arrays, *pown, lse, lse_other)


def after(x, *others):
    return lax.optimization_barrier((x, *others))[0]


def shards(n_dp, embeddings, pairings, logit_scale):
    own = embeddings[0]
    n = own.shape[0]
    group = n_dp // 8
    size = n * group
    info = pair_factors(pairings, logit_scale, size)

    def send(block, dp_xor, mod_xor):
        pairs = [(d * 4 + m, (d ^ (dp_xor * group)) * 4 + (m ^ mod_xor)) for d in range(n_dp) for m in range(4)]
        return lax.ppermute(block, ("dp", "mod"), pairs)

    def to_y(block):
        return send(block, 1, 0)

    def to_z(block):
        return send(block, 2, 0)

    def to_far(block):
        return send(block, 4, 0)

    def to_x(block):
        return send(block, 0, 2)

    def to_core(block):
        return send(block, 0, 1)

    block = own
    if group > 1:
        members = [[g * group + i for i in range(group)] for g in range(8)]
        block = lax.all_gather(own, "dp", axis=0, tiled=True, axis_index_groups=members)

    made = {}
    busy = set()
    AX = {"X": to_x, "Y": to_y, "Z": to_z, "W": to_far}

    def one(x):
        return (x, 0)

    ROUTE = CONFIG["route"]
    TIES = CONFIG["ties"]
    COST = CONFIG["cost"]

    def tied(name, x):
        t = [first(get(o)) for o in TIES.get(name, ())]
        return after(x, *t) if t else x

    def first(v):
        return v[0] if isinstance(v, (list, tuple)) else v

    def slab(v):
        return (get(v), 0)

    def get(name):
        if name in made:
            return made[name]
        assert name not in busy, "cycle"
        busy.add(name)
        if name == "a0":
            v = block
        elif name == "own":
            v = pack(get("a0"))
        elif name in ROUTE:
            parent, ax = ROUTE[name]
            v = AX[ax](tied(name, get(parent)))
        elif name in CONFIG["packs"]:
            blocks = [get(x) for x in CONFIG["packs"][name]]
            blocks[0] = tied(name, blocks[0])
            v = to_core(pack(*blocks) if len(blocks) > 1 else blocks[0])
        elif name in CONFIG["kernels"]:
            v = kernel(name)
        elif name == "lse_other":
            v = to_y(get("K3")[0])
        busy.discard(name)
        made[name] = v
        return v

    where = {}
    for pname, members in CONFIG["packs"].items():
        for i, x in enumerate(members):
            where[("c" if x[0] == "a" else "d") + x[1]] = (pname, i)

    def handle(x):
        if x in where:
            pname, i = where[x]
            return (get(pname), i)
        return (get("own" if x == "a0" else x), 0)

    KROWS, KCOLS = {}, {}
    rr, cc = [], []
    seq = list(CONFIG["kernels"])
    prevk = {}
    for k in seq:
        nr, nc = CONFIG["kernels"][k]
        prevk[k] = (list(rr), list(cc))
        rr = rr + list(nr)
        cc = cc + list(nc)
        KROWS[k], KCOLS[k] = list(rr), list(cc)
    PAIR = {"c": 1, "b": 2, "d": 3}

    def kernel(k):
        i = seq.index(k)
        old = get(seq[i - 1]) if i else None
        oldr, oldc = prevk[k]
        rows = [handle(x) for x in KROWS[k]]
        cols = [handle(x) for x in KCOLS[k]]
        rows[0] = (tied(k, rows[0][0]), rows[0][1])
        new_rows = tuple(range(len(oldr), len(KROWS[k])))
        every = tuple(range(len(KROWS[k])))
        plan = [(PAIR[x[0]], new_rows if n < len(oldc) else every) for n, x in enumerate(KCOLS[k])]
        order = None
        if i == len(seq) - 1:
            order = tuple((PAIR[x[0]] - 1) * 4 + int(x[1]) // 2 for x in KCOLS[k])
        return stats(info, size, rows, cols, plan, old, order=order, cost=COST.get(k, 4))

    for name in CONFIG["emit"]:
        get(name)
    own_block = get("own")
    lse = get(seq[-1])[0]
    lse_other = to_y(lse)
    b, c, d = ([handle(p + str(i)) for i in range(8)] for p in "bcd")

    partners = c + b + d
    pown = [c[0], b[0], d[0]]
    if group > 1:
        start = (lax.axis_index("dp") % group) * n
        pown = [lax.dynamic_slice_in_dim(x, slab * size + start, n, 0) for x, slab in pown]
        gradient, losses = whole(info, size, own, pown, lse, lse_other, partners)
    else:
        half, losses, prob, score = own_half(info, own_block, lse, partners, pown)
        odd = [x[i] for x in (c, b, d) for i in (1, 3, 5, 7)]
        gradient = other_half(info, half, prob, score, lse_other, odd)
    return gradient[None], losses


def solution(mesh):
    return jax.shard_map(
        functools.partial(shards, mesh.shape["dp"]),
        mesh=mesh,
        in_specs=(P("mod", "dp", None), P(), P()),
        out_specs=(P("mod", "dp", None), P("mod", "dp")),
        check_vma=False,
    )
```

```python
import functools
import math

import jax
import jax.numpy as jnp
from jax import lax
from jax.experimental import pallas as pl
from jax.experimental.pallas import tpu as pltpu
from jax.sharding import PartitionSpec as P

LOG2E = math.log2(math.e)
TILE = 256
NT = (((1,), (1,)), ((), ()))
SMEM = pl.BlockSpec(memory_space=pltpu.SMEM)
VMEM = pl.BlockSpec(memory_space=pltpu.VMEM)
ROUTE = {
    "a2": ("a0", "Z"),
    "a4": ("a0", "W"),
    "a1": ("a0", "Y"),
    "b0": ("a0", "X"),
    "b1": ("a1", "X"),
    "a3": ("a2", "Y"),
    "a6": ("a4", "Z"),
    "b4": ("a4", "X"),
    "a5": ("a4", "Y"),
    "b2": ("b0", "Z"),
    "b6": ("a6", "X"),
    "a7": ("a6", "Y"),
    "b3": ("b1", "Z"),
    "b5": ("a5", "X"),
    "b7": ("b6", "Y"),
}
AFTER = {
    "a6": ("b1", "b0"),
    "a5": ("a3",),
    "b2": ("a6", "b4"),
    "a7": ("a4",),
    "b3": ("b6",),
    "b5": ("b6",),
    "P4": ("b0", "b5"),
    "P1": ("a1",),
    "P3": ("b4",),
    "K2": ("b7", "b1", "a4"),
    "K1": ("a3",),
    "P5": ("a6",),
    "b1": ("own", "info"),
}
PACKS = {
    "P1": ("a2", "a4", "b0"),
    "P2": ("a6", "b1", "a7"),
    "P3": ("a5", "b4", "b2"),
    "P4": ("b3", "b5", "a3", "a1"),
    "P7": ("b6",),
    "P11": ("a0",),
    "P9": ("b7",),
}
KERNELS = {
    "K1": (("a0", "a1", "a2", "a4", "a3", "a6", "a5", "a7"), ("b0", "c0", "c2", "c4", "d0", "b6", "b2", "b4")),
    "K2": ((), ("c6", "d2")),
    "K3": ((), ("d4", "d6")),
}
COST = {
    "K1": 40,
    "K2": 40,
    "K3": 10,
}
PAIR = {"c": 1, "b": 2, "d": 3}

LIGHT = pl.CostEstimate(flops=1000, bytes_accessed=1000, transcendentals=0)


def scores(rows, cols):
    return lax.dot_general(rows, cols, NT, preferred_element_type=jnp.float32)


def factor_kernel(pairings_ref, scale_ref, out_ref):
    mine = lax.axis_index("mod")
    for m in (1, 2, 3):
        factor = jnp.float32(0.0)
        for k in range(3):
            factor = factor + jnp.where(pairings_ref[k, mine] == (mine ^ m), scale_ref[k], 0.0)
        out_ref[m - 1] = jnp.full(out_ref.shape[1:], factor, jnp.float32)
        out_ref[m + 2] = jnp.full(out_ref.shape[1:], factor * LOG2E, jnp.float32)


def pair_factors(pairings, logit_scale, size):
    return pl.pallas_call(
        factor_kernel,
        out_shape=jax.ShapeDtypeStruct((6, 8, size), jnp.float32),
        in_specs=[SMEM] * 2,
        out_specs=VMEM,
        compiler_params=pltpu.CompilerParams(vmem_limit_bytes=1 << 20),
        cost_estimate=LIGHT,
        name="pair_factors",
    )(pairings, logit_scale)


def unique(blocks):
    arrays, places = [], []
    for array, slab in blocks:
        for i, known in enumerate(arrays):
            if known is array:
                break
        else:
            i = len(arrays)
            arrays.append(array)
        places.append((i, slab))
    return arrays, places


class Placed:
    def __init__(self, ref, slab, size):
        self.ref, self.start, self.size = ref, slab * size, size

    def all(self):
        return self.ref[pl.ds(self.start, self.size), :]

    def part(self, i):
        return self.ref[pl.ds(pl.multiple_of(self.start + i * TILE, TILE), TILE), :]


def stats_kernel(size, places, n_arrays, plan, n_rows, n_old, order, n_stack, factor_ref, *refs):
    blocks = [Placed(refs[i], slab, size) for i, slab in places]
    rows, cols, stack = blocks[:n_rows], blocks[n_rows : n_rows + len(plan)], blocks[n_rows + len(plan) :]
    refs = refs[n_arrays:]
    old = refs[:2] if n_old else None
    outs = refs[2 if n_old else 0 :]
    for i, block in enumerate(stack):
        outs[-1][i * size : (i + 1) * size, :] = block.all()
    for c, (m, members) in enumerate(plan):
        scale = factor_ref[m + 2]
        if c < n_old:
            top, total = old[0][c], old[1][c]
        else:
            top = jnp.full((8, size), -1e30, jnp.float32)
            total = jnp.zeros((8, size), jnp.float32)
        block = cols[c].all()
        for r in members:

            def chunk(i, carry, r=r, block=block, scale=scale):
                top, total = carry
                s = scores(rows[r].part(i), block)
                s = s.reshape(TILE // 8, 8, size)
                new = jnp.maximum(top, jnp.max(s, 0))
                shift = new * scale
                total = total * jnp.exp2(top * scale - shift) + jnp.sum(jnp.exp2(s * scale[None] - shift[None]), 0)
                return new, total

            if size == TILE:
                top, total = chunk(0, (top, total))
            else:
                top, total = lax.fori_loop(0, size // TILE, chunk, (top, total))
        if order:
            best = jnp.max(top, 0, keepdims=True)
            total = jnp.sum(total * jnp.exp2((top - best) * scale), 0, keepdims=True)
            outs[0][order[c]] = best * scale[:1] + jnp.log2(total)
        else:
            outs[0][c] = top
            outs[1][c] = total


def stats(info, size, rows, cols, plan, old=None, order=None, stack=(), cost=4):
    arrays, places = unique(list(rows) + list(cols) + list(stack))
    width = arrays[0].shape[1]
    n = len(plan)
    n_old = old[0].shape[0] if old else 0
    state = jax.ShapeDtypeStruct((n, 8, size), jnp.float32)
    out = [jax.ShapeDtypeStruct((n, 1, size), jnp.float32)] if order else [state, state]
    if stack:
        out.append(jax.ShapeDtypeStruct((len(stack) * size, width), jnp.bfloat16))
    tiles = sum(len(members) for _, members in plan)
    used = sum(math.prod(x.shape) * 2 for x in arrays) + len(stack) * size * width * 2
    return pl.pallas_call(
        functools.partial(
            stats_kernel, size, tuple(places), len(arrays), plan, len(rows), n_old, order, len(stack)
        ),
        out_shape=tuple(out),
        in_specs=[VMEM] * (1 + len(arrays) + (2 if old else 0)),
        out_specs=tuple([VMEM] * len(out)),
        compiler_params=pltpu.CompilerParams(vmem_limit_bytes=(6 << 20) + (used if size > TILE else 0)),
        cost_estimate=pl.CostEstimate(flops=cost * tiles * size * size * width, bytes_accessed=1000, transcendentals=0),
        name="col_stats",
    )(info, *arrays, *(old or ()))


def pack_kernel(*refs):
    size = refs[0].shape[0]
    for i, ref in enumerate(refs[:-1]):
        refs[-1][i * size : (i + 1) * size, :] = ref[...]


def pack(*blocks):
    size, width = blocks[0].shape
    return pl.pallas_call(
        pack_kernel,
        out_shape=jax.ShapeDtypeStruct((len(blocks) * size, width), blocks[0].dtype),
        in_specs=[VMEM] * len(blocks),
        out_specs=VMEM,
        compiler_params=pltpu.CompilerParams(vmem_limit_bytes=(2 << 20) + (len(blocks) * size * width * 4 if size > TILE else 0)),
        cost_estimate=LIGHT,
        name="pack",
    )(*blocks)


def own_kernel(places, n_arrays, factor_ref, own_ref, lse_ref, *refs):
    blocks = [Placed(refs[i], slab, TILE) for i, slab in places]
    cols, pown = blocks[:24], blocks[24:]
    grad_ref, loss_ref, prob, score, scratch = refs[n_arrays:]
    own = own_ref[...]
    own_float = own.astype(jnp.float32)
    n = own.shape[0]
    tops, bests, totals, inverses, products = ([None] * 3 for _ in range(5))

    def held(pair, a):
        return (score if a % 2 else scratch).at[pair * 4 + a // 2]

    def score_step(pair, a):
        s = scores(own, cols[pair * 8 + a].all()) * factor_ref[pair + 3, :1]
        held(pair, a)[...] = s
        top = jnp.maximum(s[:, :128], s[:, 128:])
        tops[pair] = top if a == 0 else jnp.maximum(tops[pair], top)

    def close_scores(pair):
        bests[pair] = jnp.max(tops[pair], 1, keepdims=True)
        totals[pair] = jnp.zeros((n, 128), jnp.float32)

    def prob_step(pair, a):
        p = jnp.exp2(held(pair, a)[...] - bests[pair])
        prob[pair * 8 + a] = p
        totals[pair] = totals[pair] + p[:, :128] + p[:, 128:]

    def close_probs(pair):
        totals[pair] = jnp.sum(totals[pair], 1, keepdims=True)
        inverses[pair] = 1.0 / totals[pair]
        products[pair] = jnp.zeros(own.shape, jnp.float32)

    def weight_step(pair, a):
        p = prob[pair * 8 + a] * inverses[pair]
        if a % 2:
            prob[pair * 8 + a] = p
            return
        w = (p + jnp.exp2(held(pair, a)[...] - lse_ref[pair * 4 + a // 2])).astype(jnp.bfloat16)
        products[pair] = products[pair] + jnp.dot(
            w, cols[pair * 8 + a].all(), preferred_element_type=jnp.float32
        )

    for a in range(8):
        score_step(0, a)
    close_scores(0)
    for a in range(8):
        score_step(1, a)
        prob_step(0, a)
    close_probs(0)
    close_scores(1)
    for a in range(8):
        score_step(2, a)
        prob_step(1, a)
    close_probs(1)
    close_scores(2)
    for a in range(8):
        weight_step(0, a)
        prob_step(2, a)
    close_probs(2)
    for a in range(8):
        weight_step(1, a)
        weight_step(2, a)
    grad = jnp.zeros(own.shape, jnp.float32)
    loss = jnp.zeros((n, 1), jnp.float32)
    for pair in range(3):
        factor = factor_ref[pair, :1, :1]
        partner = pown[pair].all().astype(jnp.float32)
        grad = grad + factor * (products[pair] - 2.0 * partner)
        diagonal = factor * jnp.sum(own_float * partner, 1, keepdims=True)
        loss = loss + (bests[pair] * (1.0 / LOG2E) + jnp.log(totals[pair]) - diagonal)
    grad_ref[...] = grad
    loss_ref[...] = jnp.transpose(jnp.broadcast_to(loss, (n, 128)))[:1, :]


def own_half(info, own, lse, cols, pown):
    arrays, places = unique(cols + pown)
    n, width = own.shape
    return pl.pallas_call(
        functools.partial(own_kernel, tuple(places), len(arrays)),
        out_shape=(
            jax.ShapeDtypeStruct((n, width), jnp.float32),
            jax.ShapeDtypeStruct((1, n), jnp.float32),
            jax.ShapeDtypeStruct((24, n, TILE), jnp.float32),
            jax.ShapeDtypeStruct((12, n, TILE), jnp.float32),
        ),
        in_specs=[VMEM] * (3 + len(arrays)),
        out_specs=(VMEM,) * 4,
        scratch_shapes=[pltpu.VMEM((12, n, TILE), jnp.float32)],
        compiler_params=pltpu.CompilerParams(vmem_limit_bytes=12 * n * TILE * 4 + (6 << 20)),
        cost_estimate=LIGHT,
        name="own_half",
    )(info, own, lse, *arrays)


def other_kernel(places, n_arrays, factor_ref, half_ref, prob, score, lse_ref, *refs):
    cols = [Placed(refs[i], slab, TILE) for i, slab in places]
    grad = half_ref[...]
    for pair in range(3):
        product = jnp.zeros(half_ref.shape, jnp.float32)
        for i in range(4):
            q = jnp.exp2(score[pair * 4 + i] - lse_ref[pair * 4 + i])
            w = (prob[pair * 8 + 2 * i + 1] + q).astype(jnp.bfloat16)
            product = product + jnp.dot(w, cols[pair * 4 + i].all(), preferred_element_type=jnp.float32)
        grad = grad + factor_ref[pair, :1, :1] * product
    refs[n_arrays][...] = grad


def other_half(info, half, prob, score, lse, cols):
    arrays, places = unique(cols)
    return pl.pallas_call(
        functools.partial(other_kernel, tuple(places), len(arrays)),
        out_shape=jax.ShapeDtypeStruct(half.shape, jnp.float32),
        in_specs=[VMEM] * (5 + len(arrays)),
        out_specs=VMEM,
        compiler_params=pltpu.CompilerParams(vmem_limit_bytes=8 << 20),
        cost_estimate=LIGHT,
        name="other_half",
    )(info, half, prob, score, lse, *arrays)


def whole_kernel(size, places, n_arrays, factor_ref, own_ref, *refs):
    cols = [Placed(refs[i], slab, size) for i, slab in places]
    pown = refs[n_arrays : n_arrays + 3]
    lses = refs[n_arrays + 3 : n_arrays + 5]
    grad_ref, loss_ref, prob, colprob = refs[n_arrays + 5 :]
    groups = size // TILE
    own = own_ref[...]
    own_float = own.astype(jnp.float32)
    n = own.shape[0]
    grad = jnp.zeros(own.shape, jnp.float32)
    loss = jnp.zeros((n, 1), jnp.float32)

    def loop(f, carry):
        for a in range(8):
            carry = lax.fori_loop(0, groups, functools.partial(f, a), carry)
        return carry

    for pair in range(3):
        factor = factor_ref[pair, :1, :1]
        scale = factor_ref[pair + 3, :1, :TILE]

        def first(a, g, top, pair=pair):
            s = scores(own, cols[pair * 8 + a].part(g))
            prob[a * groups + g] = s
            return jnp.maximum(top, jnp.maximum(s[:, :128], s[:, 128:]))

        top = loop(first, jnp.full((n, 128), -1e30, jnp.float32))
        best = jnp.max(top, 1, keepdims=True) * scale[:, :1]

        def second(a, g, total, pair=pair, best=best, scale=scale):
            j = a * groups + g
            s = prob[j] * scale
            p = jnp.exp2(s - best)
            prob[j] = p
            lse = lses[a % 2][pair * 4 + a // 2, :, pl.ds(pl.multiple_of(g * TILE, TILE), TILE)]
            colprob[j] = jnp.exp2(s - lse)
            return total + p[:, :128] + p[:, 128:]

        total = jnp.sum(loop(second, jnp.zeros((n, 128), jnp.float32)), 1, keepdims=True)
        inverse = 1.0 / total

        def third(a, g, acc, pair=pair, inverse=inverse):
            j = a * groups + g
            w = (prob[j] * inverse + colprob[j]).astype(jnp.bfloat16)
            return acc + jnp.dot(w, cols[pair * 8 + a].part(g), preferred_element_type=jnp.float32)

        product = loop(third, jnp.zeros(own.shape, jnp.float32))
        partner = pown[pair][...].astype(jnp.float32)
        grad = grad + factor * (product - 2.0 * partner)
        diagonal = factor * jnp.sum(own_float * partner, 1, keepdims=True)
        loss = loss + (best * (1.0 / LOG2E) + jnp.log(total) - diagonal)
    grad_ref[...] = grad
    loss_ref[...] = jnp.transpose(jnp.broadcast_to(loss, (n, 128)))[:1, :]


def whole(info, size, own, pown, lse, lse_other, cols):
    arrays, places = unique(cols)
    n, width = own.shape
    slots = 8 * size // TILE
    scratch = pltpu.VMEM((slots, n, TILE), jnp.float32)
    need = 24 * size * width * 2 + slots * n * TILE * 8
    return pl.pallas_call(
        functools.partial(whole_kernel, size, tuple(places), len(arrays)),
        out_shape=(jax.ShapeDtypeStruct((n, width), jnp.float32), jax.ShapeDtypeStruct((1, n), jnp.float32)),
        in_specs=[VMEM] * (7 + len(arrays)),
        out_specs=(VMEM, VMEM),
        scratch_shapes=[scratch, scratch],
        compiler_params=pltpu.CompilerParams(vmem_limit_bytes=need + (6 << 20)),
        cost_estimate=LIGHT,
        name="weights_and_gradient",
    )(info, own, *arrays, *pown, lse, lse_other)


def after(x, *others):
    return lax.optimization_barrier((x, *others))[0]


def shards(n_dp, embeddings, pairings, logit_scale):
    own = embeddings[0]
    n = own.shape[0]
    group = n_dp // 8
    size = n * group
    info = pair_factors(pairings, logit_scale, size)

    def send(block, dp_xor, mod_xor):
        pairs = [(d * 4 + m, (d ^ (dp_xor * group)) * 4 + (m ^ mod_xor)) for d in range(n_dp) for m in range(4)]
        return lax.ppermute(block, ("dp", "mod"), pairs)

    def to_y(block):
        return send(block, 1, 0)

    def to_z(block):
        return send(block, 2, 0)

    def to_far(block):
        return send(block, 4, 0)

    def to_x(block):
        return send(block, 0, 2)

    def to_core(block):
        return send(block, 0, 1)

    block = own
    if group > 1:
        members = [[g * group + i for i in range(group)] for g in range(8)]
        block = lax.all_gather(own, "dp", axis=0, tiled=True, axis_index_groups=members)

    axes = {"X": to_x, "Y": to_y, "Z": to_z, "W": to_far}
    places = {}
    for pack_name, members in PACKS.items():
        for i, x in enumerate(members):
            places[("c" if x[0] == "a" else "d") + x[1]] = (pack_name, i)
    sequence = list(KERNELS)
    made = {"a0": block, "info": info}

    def released(name, x):
        waits = [get(other) for other in AFTER.get(name, ())]
        return after(x, *(w[0] if isinstance(w, tuple) else w for w in waits)) if waits else x

    def get(name):
        if name not in made:
            made[name] = make(name)
        return made[name]

    def make(name):
        if name == "own":
            return pack(get("a0"))
        if name in ROUTE:
            parent, axis = ROUTE[name]
            return axes[axis](released(name, get(parent)))
        if name in PACKS:
            blocks = [get(x) for x in PACKS[name]]
            blocks[0] = released(name, blocks[0])
            return to_core(pack(*blocks) if len(blocks) > 1 else blocks[0])
        return column_sums(name)

    def slab(x):
        if x in places:
            pack_name, i = places[x]
            return get(pack_name), i
        return get("own" if x == "a0" else x), 0

    def column_sums(name):
        step = sequence.index(name)
        old = get(sequence[step - 1]) if step else None
        rows = [x for k in sequence[: step + 1] for x in KERNELS[k][0]]
        cols = [x for k in sequence[: step + 1] for x in KERNELS[k][1]]
        every = tuple(range(len(rows)))
        new_rows = every[len(rows) - len(KERNELS[name][0]) :]
        n_old = len(cols) - len(KERNELS[name][1])
        plan = [(PAIR[x[0]], new_rows if i < n_old else every) for i, x in enumerate(cols)]
        order = None
        if step == len(sequence) - 1:
            order = tuple((PAIR[x[0]] - 1) * 4 + int(x[1]) // 2 for x in cols)
        row_slabs = [slab(x) for x in rows]
        col_slabs = [slab(x) for x in cols]
        row_slabs[0] = (released(name, row_slabs[0][0]), row_slabs[0][1])
        return tuple(stats(info, size, row_slabs, col_slabs, plan, old, order=order, cost=COST[name]))

    for name in ROUTE:
        get(name)
    own_block = get("own")
    (lse,) = get(sequence[-1])
    lse_other = to_y(lse)
    b, c, d = ([slab(p + str(i)) for i in range(8)] for p in "bcd")

    partners = c + b + d
    pown = [c[0], b[0], d[0]]
    if group > 1:
        start = (lax.axis_index("dp") % group) * n
        pown = [lax.dynamic_slice_in_dim(x, i * size + start, n, 0) for x, i in pown]
        gradient, losses = whole(info, size, own, pown, lse, lse_other, partners)
    else:
        half, losses, prob, score = own_half(info, own_block, lse, partners, pown)
        odd = [x[i] for x in (c, b, d) for i in (1, 3, 5, 7)]
        gradient = other_half(info, half, prob, score, lse_other, odd)
    return gradient[None], losses


def solution(mesh):
    return jax.shard_map(
        functools.partial(shards, mesh.shape["dp"]),
        mesh=mesh,
        in_specs=(P("mod", "dp", None), P(), P()),
        out_specs=(P("mod", "dp", None), P("mod", "dp")),
        check_vma=False,
    )
```

```python
import functools
import math

import jax
import jax.numpy as jnp
from jax import lax
from jax.experimental import pallas as pl
from jax.experimental.pallas import tpu as pltpu
from jax.sharding import PartitionSpec as P

LOG2E = math.log2(math.e)
TILE = 256
NT = (((1,), (1,)), ((), ()))
SMEM = pl.BlockSpec(memory_space=pltpu.SMEM)
VMEM = pl.BlockSpec(memory_space=pltpu.VMEM)
ROUTE = {
    "a2": ("a0", "Z"),
    "a4": ("a0", "W"),
    "a1": ("a0", "Y"),
    "a5": ("a4", "Y"),
    "b1": ("a1", "X"),
    "a3": ("a2", "Y"),
    "a6": ("a4", "Z"),
    "b4": ("a4", "X"),
    "b0": ("a0", "X"),
    "b2": ("b0", "Z"),
    "b6": ("a6", "X"),
    "a7": ("a6", "Y"),
    "b3": ("b1", "Z"),
    "b5": ("a5", "X"),
    "b7": ("b6", "Y"),
}
AFTER = {
    "a6": ("b1", "b0"),
    "a5": ("a3",),
    "b2": ("a6", "b4"),
    "a7": ("a4",),
    "b3": ("b6",),
    "b5": ("b6",),
    "P4": ("b0", "b5"),
    "P1": ("a1",),
    "K1": ("a3",),
    "P5": ("a6",),
    "b1": ("own", "info"),
    "P9": ("K3",),
    "P3": ("a4", "info"),
}
PACKS = {
    "P1": ("a2", "a4", "b0"),
    "P2": ("a6", "b1", "a7", "b6", "a5", "b4", "b2"),
    "P4": ("b3", "b5", "a3", "a1"),
    "P11": ("a0",),
    "P9": ("b7",),
}
KERNELS = {
    "K1": (("a0", "a1", "a2", "a4", "a3", "a6", "a5", "a7"), ("b0", "c0", "c2", "c4", "d0", "b6", "b2", "b4")),
    "K3": ((), ("c6", "d2", "d4", "d6")),
}
COST = {
    "K1": 40,
    "K3": 20,
}
PAIR = {"c": 1, "b": 2, "d": 3}

LIGHT = pl.CostEstimate(flops=1000, bytes_accessed=1000, transcendentals=0)


def scores(rows, cols):
    return lax.dot_general(rows, cols, NT, preferred_element_type=jnp.float32)


def factor_kernel(pairings_ref, scale_ref, out_ref):
    mine = lax.axis_index("mod")
    for m in (1, 2, 3):
        factor = jnp.float32(0.0)
        for k in range(3):
            factor = factor + jnp.where(pairings_ref[k, mine] == (mine ^ m), scale_ref[k], 0.0)
        out_ref[m - 1] = jnp.full(out_ref.shape[1:], factor, jnp.float32)
        out_ref[m + 2] = jnp.full(out_ref.shape[1:], factor * LOG2E, jnp.float32)


def pair_factors(pairings, logit_scale, size):
    return pl.pallas_call(
        factor_kernel,
        out_shape=jax.ShapeDtypeStruct((6, 8, size), jnp.float32),
        in_specs=[SMEM] * 2,
        out_specs=VMEM,
        compiler_params=pltpu.CompilerParams(vmem_limit_bytes=1 << 20),
        cost_estimate=LIGHT,
        name="pair_factors",
    )(pairings, logit_scale)


def unique(blocks):
    arrays, places = [], []
    for array, slab in blocks:
        for i, known in enumerate(arrays):
            if known is array:
                break
        else:
            i = len(arrays)
            arrays.append(array)
        places.append((i, slab))
    return arrays, places


class Placed:
    def __init__(self, ref, slab, size):
        self.ref, self.start, self.size = ref, slab * size, size

    def all(self):
        return self.ref[pl.ds(self.start, self.size), :]

    def part(self, i):
        return self.ref[pl.ds(pl.multiple_of(self.start + i * TILE, TILE), TILE), :]


def stats_kernel(size, places, n_arrays, plan, n_rows, n_old, order, n_stack, factor_ref, *refs):
    blocks = [Placed(refs[i], slab, size) for i, slab in places]
    rows, cols, stack = blocks[:n_rows], blocks[n_rows : n_rows + len(plan)], blocks[n_rows + len(plan) :]
    refs = refs[n_arrays:]
    old = refs[:2] if n_old else None
    outs = refs[2 if n_old else 0 :]
    for i, block in enumerate(stack):
        outs[-1][i * size : (i + 1) * size, :] = block.all()
    for c, (m, members) in enumerate(plan):
        scale = factor_ref[m + 2]
        if c < n_old:
            top, total = old[0][c], old[1][c]
        else:
            top = jnp.full((8, size), -1e30, jnp.float32)
            total = jnp.zeros((8, size), jnp.float32)
        block = cols[c].all()
        for r in members:

            def chunk(i, carry, r=r, block=block, scale=scale):
                top, total = carry
                s = scores(rows[r].part(i), block)
                s = s.reshape(TILE // 8, 8, size)
                new = jnp.maximum(top, jnp.max(s, 0))
                shift = new * scale
                total = total * jnp.exp2(top * scale - shift) + jnp.sum(jnp.exp2(s * scale[None] - shift[None]), 0)
                return new, total

            if size == TILE:
                top, total = chunk(0, (top, total))
            else:
                top, total = lax.fori_loop(0, size // TILE, chunk, (top, total))
        if order:
            best = jnp.max(top, 0, keepdims=True)
            total = jnp.sum(total * jnp.exp2((top - best) * scale), 0, keepdims=True)
            outs[0][order[c]] = best * scale[:1] + jnp.log2(total)
        else:
            outs[0][c] = top
            outs[1][c] = total


def stats(info, size, rows, cols, plan, old=None, order=None, stack=(), cost=4):
    arrays, places = unique(list(rows) + list(cols) + list(stack))
    width = arrays[0].shape[1]
    n = len(plan)
    n_old = old[0].shape[0] if old else 0
    state = jax.ShapeDtypeStruct((n, 8, size), jnp.float32)
    out = [jax.ShapeDtypeStruct((n, 1, size), jnp.float32)] if order else [state, state]
    if stack:
        out.append(jax.ShapeDtypeStruct((len(stack) * size, width), jnp.bfloat16))
    tiles = sum(len(members) for _, members in plan)
    used = sum(math.prod(x.shape) * 2 for x in arrays) + len(stack) * size * width * 2
    return pl.pallas_call(
        functools.partial(
            stats_kernel, size, tuple(places), len(arrays), plan, len(rows), n_old, order, len(stack)
        ),
        out_shape=tuple(out),
        in_specs=[VMEM] * (1 + len(arrays) + (2 if old else 0)),
        out_specs=tuple([VMEM] * len(out)),
        compiler_params=pltpu.CompilerParams(vmem_limit_bytes=(6 << 20) + (used if size > TILE else 0)),
        cost_estimate=pl.CostEstimate(flops=cost * tiles * size * size * width, bytes_accessed=1000, transcendentals=0),
        name="col_stats",
    )(info, *arrays, *(old or ()))


def pack_kernel(*refs):
    size = refs[0].shape[0]
    for i, ref in enumerate(refs[:-1]):
        refs[-1][i * size : (i + 1) * size, :] = ref[...]


def pack(*blocks):
    size, width = blocks[0].shape
    return pl.pallas_call(
        pack_kernel,
        out_shape=jax.ShapeDtypeStruct((len(blocks) * size, width), blocks[0].dtype),
        in_specs=[VMEM] * len(blocks),
        out_specs=VMEM,
        compiler_params=pltpu.CompilerParams(vmem_limit_bytes=(2 << 20) + (len(blocks) * size * width * 4 if size > TILE else 0)),
        cost_estimate=LIGHT,
        name="pack",
    )(*blocks)


def own_kernel(places, n_arrays, factor_ref, own_ref, lse_ref, *refs):
    blocks = [Placed(refs[i], slab, TILE) for i, slab in places]
    cols, pown = blocks[:24], blocks[24:]
    grad_ref, loss_ref, prob, score, scratch = refs[n_arrays:]
    own = own_ref[...]
    own_float = own.astype(jnp.float32)
    n = own.shape[0]
    tops, bests, totals, inverses, products = ([None] * 3 for _ in range(5))

    def held(pair, a):
        return (score if a % 2 else scratch).at[pair * 4 + a // 2]

    def score_step(pair, a):
        s = scores(own, cols[pair * 8 + a].all()) * factor_ref[pair + 3, :1]
        held(pair, a)[...] = s
        top = jnp.maximum(s[:, :128], s[:, 128:])
        tops[pair] = top if a == 0 else jnp.maximum(tops[pair], top)

    def close_scores(pair):
        bests[pair] = jnp.max(tops[pair], 1, keepdims=True)
        totals[pair] = jnp.zeros((n, 128), jnp.float32)

    def prob_step(pair, a):
        p = jnp.exp2(held(pair, a)[...] - bests[pair])
        prob[pair * 8 + a] = p
        totals[pair] = totals[pair] + p[:, :128] + p[:, 128:]

    def close_probs(pair):
        totals[pair] = jnp.sum(totals[pair], 1, keepdims=True)
        inverses[pair] = 1.0 / totals[pair]
        products[pair] = jnp.zeros(own.shape, jnp.float32)

    def weight_step(pair, a):
        p = prob[pair * 8 + a] * inverses[pair]
        if a % 2:
            prob[pair * 8 + a] = p
            return
        w = (p + jnp.exp2(held(pair, a)[...] - lse_ref[pair * 4 + a // 2])).astype(jnp.bfloat16)
        products[pair] = products[pair] + jnp.dot(
            w, cols[pair * 8 + a].all(), preferred_element_type=jnp.float32
        )

    for a in range(8):
        score_step(0, a)
    close_scores(0)
    for a in range(8):
        score_step(1, a)
        prob_step(0, a)
    close_probs(0)
    close_scores(1)
    for a in range(8):
        score_step(2, a)
        prob_step(1, a)
    close_probs(1)
    close_scores(2)
    for a in range(8):
        weight_step(0, a)
        prob_step(2, a)
    close_probs(2)
    for a in range(8):
        weight_step(1, a)
        weight_step(2, a)
    grad = jnp.zeros(own.shape, jnp.float32)
    loss = jnp.zeros((n, 1), jnp.float32)
    for pair in range(3):
        factor = factor_ref[pair, :1, :1]
        partner = pown[pair].all().astype(jnp.float32)
        grad = grad + factor * (products[pair] - 2.0 * partner)
        diagonal = factor * jnp.sum(own_float * partner, 1, keepdims=True)
        loss = loss + (bests[pair] * (1.0 / LOG2E) + jnp.log(totals[pair]) - diagonal)
    grad_ref[...] = grad
    loss_ref[...] = jnp.transpose(jnp.broadcast_to(loss, (n, 128)))[:1, :]


def own_half(info, own, lse, cols, pown):
    arrays, places = unique(cols + pown)
    n, width = own.shape
    return pl.pallas_call(
        functools.partial(own_kernel, tuple(places), len(arrays)),
        out_shape=(
            jax.ShapeDtypeStruct((n, width), jnp.float32),
            jax.ShapeDtypeStruct((1, n), jnp.float32),
            jax.ShapeDtypeStruct((24, n, TILE), jnp.float32),
            jax.ShapeDtypeStruct((12, n, TILE), jnp.float32),
        ),
        in_specs=[VMEM] * (3 + len(arrays)),
        out_specs=(VMEM,) * 4,
        scratch_shapes=[pltpu.VMEM((12, n, TILE), jnp.float32)],
        compiler_params=pltpu.CompilerParams(vmem_limit_bytes=12 * n * TILE * 4 + (6 << 20)),
        cost_estimate=LIGHT,
        name="own_half",
    )(info, own, lse, *arrays)


def other_kernel(places, n_arrays, factor_ref, half_ref, prob, score, lse_ref, *refs):
    cols = [Placed(refs[i], slab, TILE) for i, slab in places]
    grad = half_ref[...]
    for pair in range(3):
        product = jnp.zeros(half_ref.shape, jnp.float32)
        for i in range(4):
            q = jnp.exp2(score[pair * 4 + i] - lse_ref[pair * 4 + i])
            w = (prob[pair * 8 + 2 * i + 1] + q).astype(jnp.bfloat16)
            product = product + jnp.dot(w, cols[pair * 4 + i].all(), preferred_element_type=jnp.float32)
        grad = grad + factor_ref[pair, :1, :1] * product
    refs[n_arrays][...] = grad


def other_half(info, half, prob, score, lse, cols):
    arrays, places = unique(cols)
    return pl.pallas_call(
        functools.partial(other_kernel, tuple(places), len(arrays)),
        out_shape=jax.ShapeDtypeStruct(half.shape, jnp.float32),
        in_specs=[VMEM] * (5 + len(arrays)),
        out_specs=VMEM,
        compiler_params=pltpu.CompilerParams(vmem_limit_bytes=8 << 20),
        cost_estimate=LIGHT,
        name="other_half",
    )(info, half, prob, score, lse, *arrays)


def whole_kernel(size, places, n_arrays, factor_ref, own_ref, *refs):
    cols = [Placed(refs[i], slab, size) for i, slab in places]
    pown = refs[n_arrays : n_arrays + 3]
    lses = refs[n_arrays + 3 : n_arrays + 5]
    grad_ref, loss_ref, prob, colprob = refs[n_arrays + 5 :]
    groups = size // TILE
    own = own_ref[...]
    own_float = own.astype(jnp.float32)
    n = own.shape[0]
    grad = jnp.zeros(own.shape, jnp.float32)
    loss = jnp.zeros((n, 1), jnp.float32)

    def loop(f, carry):
        for a in range(8):
            carry = lax.fori_loop(0, groups, functools.partial(f, a), carry)
        return carry

    for pair in range(3):
        factor = factor_ref[pair, :1, :1]
        scale = factor_ref[pair + 3, :1, :TILE]

        def first(a, g, top, pair=pair):
            s = scores(own, cols[pair * 8 + a].part(g))
            prob[a * groups + g] = s
            return jnp.maximum(top, jnp.maximum(s[:, :128], s[:, 128:]))

        top = loop(first, jnp.full((n, 128), -1e30, jnp.float32))
        best = jnp.max(top, 1, keepdims=True) * scale[:, :1]

        def second(a, g, total, pair=pair, best=best, scale=scale):
            j = a * groups + g
            s = prob[j] * scale
            p = jnp.exp2(s - best)
            prob[j] = p
            lse = lses[a % 2][pair * 4 + a // 2, :, pl.ds(pl.multiple_of(g * TILE, TILE), TILE)]
            colprob[j] = jnp.exp2(s - lse)
            return total + p[:, :128] + p[:, 128:]

        total = jnp.sum(loop(second, jnp.zeros((n, 128), jnp.float32)), 1, keepdims=True)
        inverse = 1.0 / total

        def third(a, g, acc, pair=pair, inverse=inverse):
            j = a * groups + g
            w = (prob[j] * inverse + colprob[j]).astype(jnp.bfloat16)
            return acc + jnp.dot(w, cols[pair * 8 + a].part(g), preferred_element_type=jnp.float32)

        product = loop(third, jnp.zeros(own.shape, jnp.float32))
        partner = pown[pair][...].astype(jnp.float32)
        grad = grad + factor * (product - 2.0 * partner)
        diagonal = factor * jnp.sum(own_float * partner, 1, keepdims=True)
        loss = loss + (best * (1.0 / LOG2E) + jnp.log(total) - diagonal)
    grad_ref[...] = grad
    loss_ref[...] = jnp.transpose(jnp.broadcast_to(loss, (n, 128)))[:1, :]


def whole(info, size, own, pown, lse, lse_other, cols):
    arrays, places = unique(cols)
    n, width = own.shape
    slots = 8 * size // TILE
    scratch = pltpu.VMEM((slots, n, TILE), jnp.float32)
    need = 24 * size * width * 2 + slots * n * TILE * 8
    return pl.pallas_call(
        functools.partial(whole_kernel, size, tuple(places), len(arrays)),
        out_shape=(jax.ShapeDtypeStruct((n, width), jnp.float32), jax.ShapeDtypeStruct((1, n), jnp.float32)),
        in_specs=[VMEM] * (7 + len(arrays)),
        out_specs=(VMEM, VMEM),
        scratch_shapes=[scratch, scratch],
        compiler_params=pltpu.CompilerParams(vmem_limit_bytes=need + (6 << 20)),
        cost_estimate=LIGHT,
        name="weights_and_gradient",
    )(info, own, *arrays, *pown, lse, lse_other)


def after(x, *others):
    return lax.optimization_barrier((x, *others))[0]


def shards(n_dp, embeddings, pairings, logit_scale):
    own = embeddings[0]
    n = own.shape[0]
    group = n_dp // 8
    size = n * group
    info = pair_factors(pairings, logit_scale, size)

    def send(block, dp_xor, mod_xor):
        pairs = [(d * 4 + m, (d ^ (dp_xor * group)) * 4 + (m ^ mod_xor)) for d in range(n_dp) for m in range(4)]
        return lax.ppermute(block, ("dp", "mod"), pairs)

    def to_y(block):
        return send(block, 1, 0)

    def to_z(block):
        return send(block, 2, 0)

    def to_far(block):
        return send(block, 4, 0)

    def to_x(block):
        return send(block, 0, 2)

    def to_core(block):
        return send(block, 0, 1)

    block = own
    if group > 1:
        members = [[g * group + i for i in range(group)] for g in range(8)]
        block = lax.all_gather(own, "dp", axis=0, tiled=True, axis_index_groups=members)

    axes = {"X": to_x, "Y": to_y, "Z": to_z, "W": to_far}
    places = {}
    for pack_name, members in PACKS.items():
        for i, x in enumerate(members):
            places[("c" if x[0] == "a" else "d") + x[1]] = (pack_name, i)
    sequence = list(KERNELS)
    made = {"a0": block, "info": info}

    def released(name, x):
        waits = [get(other) for other in AFTER.get(name, ())]
        return after(x, *(w[0] if isinstance(w, tuple) else w for w in waits)) if waits else x

    def get(name):
        if name not in made:
            made[name] = make(name)
        return made[name]

    def make(name):
        if name == "own":
            return pack(get("a0"))
        if name in ROUTE:
            parent, axis = ROUTE[name]
            return axes[axis](released(name, get(parent)))
        if name in PACKS:
            blocks = [get(x) for x in PACKS[name]]
            blocks[0] = released(name, blocks[0])
            return to_core(pack(*blocks) if len(blocks) > 1 else blocks[0])
        return column_sums(name)

    def slab(x):
        if x in places:
            pack_name, i = places[x]
            return get(pack_name), i
        return get("own" if x == "a0" else x), 0

    def column_sums(name):
        step = sequence.index(name)
        old = get(sequence[step - 1]) if step else None
        rows = [x for k in sequence[: step + 1] for x in KERNELS[k][0]]
        cols = [x for k in sequence[: step + 1] for x in KERNELS[k][1]]
        every = tuple(range(len(rows)))
        new_rows = every[len(rows) - len(KERNELS[name][0]) :]
        n_old = len(cols) - len(KERNELS[name][1])
        plan = [(PAIR[x[0]], new_rows if i < n_old else every) for i, x in enumerate(cols)]
        order = None
        if step == len(sequence) - 1:
            order = tuple((PAIR[x[0]] - 1) * 4 + int(x[1]) // 2 for x in cols)
        row_slabs = [slab(x) for x in rows]
        col_slabs = [slab(x) for x in cols]
        row_slabs[0] = (released(name, row_slabs[0][0]), row_slabs[0][1])
        return tuple(stats(info, size, row_slabs, col_slabs, plan, old, order=order, cost=COST[name]))

    for name in ROUTE:
        get(name)
    own_block = get("own")
    (lse,) = get(sequence[-1])
    lse_other = to_y(lse)
    b, c, d = ([slab(p + str(i)) for i in range(8)] for p in "bcd")

    partners = c + b + d
    pown = [c[0], b[0], d[0]]
    if group > 1:
        start = (lax.axis_index("dp") % group) * n
        pown = [lax.dynamic_slice_in_dim(x, i * size + start, n, 0) for x, i in pown]
        gradient, losses = whole(info, size, own, pown, lse, lse_other, partners)
    else:
        half, losses, prob, score = own_half(info, own_block, lse, partners, pown)
        odd = [x[i] for x in (c, b, d) for i in (1, 3, 5, 7)]
        gradient = other_half(info, half, prob, score, lse_other, odd)
    return gradient[None], losses


def solution(mesh):
    return jax.shard_map(
        functools.partial(shards, mesh.shape["dp"]),
        mesh=mesh,
        in_specs=(P("mod", "dp", None), P(), P()),
        out_specs=(P("mod", "dp", None), P("mod", "dp")),
        check_vma=False,
    )
```
